128 devices in a mesh: worker: 8 (over y, x_hi), fsdp: 16 (over x_lo, z, core).
Axes of the slice: x: 4 (x_hi: 2, x_lo: 2; x = x_hi * 2 + x_lo), y: 4, z: 4, core: 2. Of those that a mesh axis runs over, the one named last changes fastest.
Arguments:
- hidden: bfloat16 [49152, 8192], P(('worker', 'fsdp')), may hold values from -6 to 6
- key_grad: bfloat16 [49152, 1024], P(('worker', 'fsdp')), may hold values from -6 to 6
- local_weight: float32 [8, 8192, 1024], P('worker', 'fsdp'), may hold values from -3 to 3
- global_weight: float32 [8192, 1024], P('fsdp'), may hold values from -3 to 3
- momentum: float32 [8192, 1024], P('fsdp'), may hold values from -3 to 3
Outputs:
- keys: bfloat16 [49152, 1024], P(('worker', 'fsdp'))
- hidden_grad: bfloat16 [49152, 8192], P(('worker', 'fsdp'))
- merged_weight: float32 [8, 8192, 1024], P('worker', 'fsdp')
- global_new: float32 [8192, 1024], P('fsdp')
- momentum_new: float32 [8192, 1024], P('fsdp')
The draws below stay inside these ranges and needn't reach their ends.
All inputs are finite; a program needn't handle non-finite values.
Results may differ from the reference program's by a relative error of at most 0.0085.
Values may be sent and summed in bfloat16 or wider, within the bound.
A program may use at most 192 MiB of HBM per device.

```python
import jax
import jax.numpy as jnp
from jax import lax

D = 8192
KV = 1024
TOK_DEV = 384
TOKENS = 49152
N_WORKER = 8
N_FSDP = 16


def levels(rng, dims, split, low, high):
    gain = 1.0
    for axis_at, shards_of in split:
        steps = jax.random.uniform(jax.random.fold_in(jax.random.fold_in(rng, 6), axis_at), (shards_of,), jnp.float32, low / len(split), high / len(split))
        gain = gain * jnp.repeat(jnp.exp(steps), dims[axis_at] // shards_of).reshape((-1,) + (1,) * (len(dims) - 1 - axis_at))
    return gain


def gaussian(own_key, dims, scale, most, cuts=(), dtype=jnp.bfloat16):
    level = levels(own_key, dims, cuts, -0.22, 0.18) if cuts else 1.0
    array = jax.random.normal(own_key, dims, jnp.float32) * scale * level
    return jnp.minimum(jnp.maximum(array, -most), most).astype(dtype)


def setup_inputs(seed: int = 0) -> dict:
    key_list = jax.random.split(jax.random.key(seed), 6)
    hidden = gaussian(key_list[0], (TOKENS, D), 1.0, 6.0, ((0, 128),))
    key_grad = gaussian(key_list[1], (TOKENS, KV), 1.0, 6.0, ((0, 128),))
    local_weight = gaussian(key_list[2], (N_WORKER, D, KV), 0.5, 3.0, ((0, 8), (1, 16)), jnp.float32)
    global_weight = gaussian(key_list[3], (D, KV), 0.5, 3.0, ((0, 16),), jnp.float32)
    momentum = gaussian(key_list[4], (D, KV), 0.5, 3.0, ((0, 16),), jnp.float32)
    return dict(hidden=hidden, key_grad=key_grad, local_weight=local_weight, global_weight=global_weight, momentum=momentum)


momentum_coef = 0.9
outer_rate = 0.7
inner_rate = 0.3
mix_weight = 0.5


def reference(hidden, key_grad, local_weight, global_weight, momentum):
    group = TOK_DEV * N_FSDP
    scale = D ** -0.5
    blocks_hidden = hidden.reshape(N_WORKER, N_FSDP, TOK_DEV, D)
    blocks_grad = key_grad.reshape(N_WORKER, N_FSDP, TOK_DEV, KV)

    def replica(packed):
        block_h, block_g, weight = packed
        weight_bf = weight.astype(jnp.bfloat16)
        flat_h = block_h.reshape(group, D)
        flat_g = block_g.reshape(group, KV)
        keys = (jnp.dot(flat_h, weight_bf, preferred_element_type=jnp.float32) * scale).astype(jnp.bfloat16)
        back = lax.dot_general(flat_g, weight_bf, (((1,), (1,)), ((), ())), preferred_element_type=jnp.float32)
        back = (back * scale).astype(jnp.bfloat16)

        def accumulate(total, pair):
            part_h, part_g = pair
            term = lax.dot_general(part_h, part_g, (((0,), (0,)), ((), ())), preferred_element_type=jnp.float32)
            term = (term * scale).astype(jnp.bfloat16).astype(jnp.float32)
            return total + term, None

        grad, _ = lax.scan(accumulate, jnp.zeros((D, KV), jnp.float32), (block_h, block_g))
        return keys, back, grad

    keys, back, grads = lax.map(replica, (blocks_hidden, blocks_grad, local_weight))
    delta = jnp.mean(global_weight[None] - local_weight, axis=0)
    momentum_new = momentum_coef * momentum + delta
    global_new = global_weight - outer_rate * (momentum_coef * momentum_new + delta)
    merged = mix_weight * (local_weight - inner_rate * grads) + (1.0 - mix_weight) * global_new[None]
    return keys.reshape(TOKENS, KV), back.reshape(TOKENS, D), merged, global_new, momentum_new
```

```python
import jax
import jax.numpy as jnp
from jax import lax
from jax.experimental import pallas as pl
from jax.experimental.pallas import tpu as pltpu
from jax.sharding import PartitionSpec as P

D = 8192
KV = 1024
TOK = 384
ROWS = 512
SCALE = D ** (-0.5)
MESH = pl.DeviceIdType.MESH

momentum_coef = 0.9
outer_rate = 0.7
inner_rate = 0.3
mix_weight = 0.5

AX = 320
RX = 288
ZERO, PLUS, MINUS, FAR = 0, 1, 2, 3


def slot(dx, dz):
    return dx * 4 + dz


def kernel(
    hid, kg, loc, glo, mom,
    o_keys, o_back, o_merged, o_glob, o_mom,
    W, H, K, G, acc, acc_in, keys_st, back_st, L, GL, M, DF, RY, A, RXH, DL,
    x_zpart, x_last, half_x, half_z, full_x, full_z,
    ssem, rsem, lsem,
):
    f32, bf16 = jnp.float32, jnp.bfloat16
    w, f = lax.axis_index("worker"), lax.axis_index("fsdp")
    y, xh = w // 2, lax.rem(w, 2)
    xl, z, c = f // 8, lax.rem(f, 8) // 2, lax.rem(f, 2)

    def dev(y_, xh_, xl_, z_, c_):
        return (y_ * 2 + xh_, xl_ * 8 + z_ * 2 + c_)

    z_up, z_down = lax.rem(z + 1, 4), lax.rem(z + 3, 4)
    up, down = dev(y, xh, xl, z_up, c), dev(y, xh, xl, z_down, c)
    pair = dev(y, xh, 1 - xl, z, c)
    core = dev(y, xh, xl, z, 1 - c)
    cross = dev(y, 1 - xh, xl, z, c)
    ys = [dev(lax.rem(y + k, 4), xh, xl, z, c) for k in (1, 2, 3)]

    counts = {"remote": 0, "local": 0}
    sent = []

    def send(src, dst, to, keep=True):
        i = counts["remote"]
        counts["remote"] += 1
        copy = pltpu.make_async_remote_copy(
            src_ref=src, dst_ref=dst, send_sem=ssem.at[i], recv_sem=rsem.at[i],
            device_id=to, device_id_type=MESH,
        )
        copy.start()
        if keep:
            sent.append(copy)
        return copy

    def move(src, dst):
        i = counts["local"]
        counts["local"] += 1
        copy = pltpu.make_async_copy(src, dst, lsem.at[i])
        copy.start()
        return copy

    def columns(s, parity):
        dx, dz = divmod(s, 4)
        shift = (0, 1, 3, 2)[dz]
        chip = (xl + dx - 2 * xl * dx) * 4 + lax.rem(z + shift, 4)
        return pl.ds(pl.multiple_of((chip * 2 + parity) * ROWS, ROWS), ROWS)

    ld_loc = [move(loc.at[pl.ds(AX, ROWS - AX)], L.at[pl.ds(AX, ROWS - AX)]),
              move(loc.at[pl.ds(0, AX)], L.at[pl.ds(0, AX)])]
    ld_kg = move(kg, K.at[pl.ds(0, TOK)])
    ld_glo = move(glo, GL)
    order = [slot(1, FAR), slot(0, FAR), slot(1, PLUS), slot(1, MINUS),
             slot(0, PLUS), slot(0, MINUS), slot(1, ZERO), slot(0, ZERO)]

    barrier = pltpu.get_barrier_semaphore()
    partners = [up, down, pair, core, cross, *ys]
    for d in partners:
        pl.semaphore_signal(barrier, inc=1, device_id=d, device_id_type=MESH)
    pl.semaphore_wait(barrier, len(partners))

    def rounded(lo, n):
        @pl.loop(0, n // 32)
        def _(r):
            at = pl.ds(pl.multiple_of(lo + r * 32, 32), 32)
            W[slot(0, ZERO), at, :] = L[at, :].astype(bf16)

    aX, aZ = pl.ds(0, AX), pl.ds(AX, ROWS - AX)
    hX = (pl.ds(0, AX // 2), pl.ds(AX // 2, AX // 2))
    nz = (ROWS - AX) // 2
    hZ = (pl.ds(AX, nz), pl.ds(AX + nz, nz))
    own = slot(0, ZERO)

    def w_send(src, dst, rows, to):
        return send(W.at[src, rows], W.at[dst, rows], to)

    ld_loc[0].wait()
    rounded(AX, ROWS - AX)
    up_z = w_send(own, slot(0, MINUS), aZ, up)
    down_z = w_send(own, slot(0, PLUS), aZ, down)
    ld_loc[1].wait()
    rounded(0, AX)
    pair_x = w_send(own, slot(1, ZERO), aX, pair)
    up_x = w_send(own, slot(0, MINUS), aX, up)
    down_x = w_send(own, slot(0, PLUS), aX, down)
    pair_z = w_send(own, slot(1, ZERO), aZ, pair)

    sw_kg = send(kg, K.at[pl.ds(TOK, TOK)], core)
    sw_hid, ld_hid = {}, {}
    for s in order:
        sw_hid[s] = send(hid.at[:, columns(s, 1 - c)], H.at[s, pl.ds(TOK, TOK)], core)
        ld_hid[s] = move(hid.at[:, columns(s, c)], H.at[s, pl.ds(0, TOK)])
    ld_mom = move(mom, M)

    ld_glo.wait()

    @pl.loop(0, ROWS // 32)
    def _(r):
        at = pl.ds(pl.multiple_of(r * 32, 32), 32)
        DF[at, :] = (GL[at, :] - L[at, :]).astype(bf16)

    def quarter(q):
        return pl.ds(pl.multiple_of(q * 128, 128), 128)

    y_parts = [send(DF.at[quarter(lax.rem(y + k, 4))], RY.at[k - 1], ys[k - 1]) for k in (1, 2, 3)]

    ld_kg.wait()
    sw_kg.wait_recv()

    def product(s):
        ld_hid[s].wait()
        sw_hid[s].wait_recv()

        @pl.loop(0, KV // 256)
        def _(j):
            at = pl.ds(pl.multiple_of(j * 256, 256), 256)
            term = lax.dot_general(H[s], K[:, at], (((0,), (0,)), ((), ())), preferred_element_type=f32)
            G[s, :, at] = (term * SCALE).astype(bf16)

    state = {"first": True, "n": 0, "out": {}}

    def forward(s):
        first = state["first"]
        state["first"] = False

        @pl.loop(0, KV // 256)
        def _(j):
            at = pl.ds(pl.multiple_of(j * 256, 256), 256)
            part = jnp.dot(H[s], W[s, :, at], preferred_element_type=f32)
            if first:
                acc[:, at] = part
            else:
                acc[:, at] += part

        n = state["n"]
        state["n"] += 1
        b = n % 2
        if n >= 2:
            mine, theirs = state["out"][n - 2]
            mine.wait()
            theirs.wait_send()

        @pl.loop(0, ROWS // 256)
        def _(j):
            at = pl.ds(pl.multiple_of(j * 256, 256), 256)
            back = lax.dot_general(K[...], W[s, at, :], (((1,), (1,)), ((), ())), preferred_element_type=f32)
            back_st[b, :, at] = (back * SCALE).astype(bf16)

        cols = columns(s, c)
        mine = move(back_st.at[b, pl.ds(0, TOK)], o_back.at[:, cols])
        theirs = send(back_st.at[b, pl.ds(TOK, TOK)], o_back.at[:, cols], core, keep=False)
        state["out"][n] = (mine, theirs)

    for s in order[:6]:
        product(s)
    up_z.wait_recv()
    down_z.wait_recv()
    far_z = (w_send(slot(0, MINUS), slot(0, FAR), hZ[0], up), w_send(slot(0, PLUS), slot(0, FAR), hZ[1], down))
    pair_zm = w_send(slot(0, MINUS), slot(1, MINUS), aZ, pair)
    pair_zp = w_send(slot(0, PLUS), slot(1, PLUS), aZ, pair)
    for s in order[6:]:
        product(s)
    pair_x.wait_recv()
    up_px = w_send(slot(1, ZERO), slot(1, MINUS), aX, up)
    down_px = w_send(slot(1, ZERO), slot(1, PLUS), aX, down)
    forward(own)

    for copy in y_parts:
        copy.wait_recv()

    @pl.loop(0, 128 // 32)
    def _(r):
        at = pl.ds(pl.multiple_of(r * 32, 32), 32)
        mine = DF[pl.ds(pl.multiple_of(y * 128 + r * 32, 32), 32), :].astype(f32)
        total = (mine + RY[0, at, :].astype(f32)) + (RY[1, at, :].astype(f32) + RY[2, at, :].astype(f32))
        A[at, :] = total.astype(bf16)

    x_sum = send(A, RXH, cross)

    up_x.wait_recv()
    down_x.wait_recv()
    far_x = (w_send(slot(0, MINUS), slot(0, FAR), hX[0], up), w_send(slot(0, PLUS), slot(0, FAR), hX[1], down))
    forward(slot(0, PLUS))
    forward(slot(0, MINUS))
    for copy in far_z:
        copy.wait_recv()
    pair_z2 = w_send(slot(0, FAR), slot(1, FAR), aZ, pair)
    pair_z.wait_recv()
    forward(slot(1, ZERO))

    x_sum.wait_recv()

    @pl.loop(0, 128 // 32)
    def _(r):
        at = pl.ds(pl.multiple_of(r * 32, 32), 32)
        total = A[at, :].astype(f32) + RXH[at, :].astype(f32)
        DL[pl.ds(pl.multiple_of(y * 128 + r * 32, 32), 32), :] = (total * 0.125).astype(bf16)

    y_back = [send(DL.at[quarter(y)], DL.at[quarter(y)], ys[k - 1]) for k in (1, 2, 3)]

    up_px.wait_recv()
    down_px.wait_recv()
    far_px = (w_send(slot(1, MINUS), slot(1, FAR), hX[0], up), w_send(slot(1, PLUS), slot(1, FAR), hX[1], down))

    gX, gZ = pl.ds(0, RX), pl.ds(RX, ROWS - RX)
    gx2, gz2 = RX // 2, (ROWS - RX) // 2
    x_parts = [send(G.at[slot(1, dz), gZ], x_zpart.at[dz], pair) for dz in (FAR, PLUS, MINUS, ZERO)]
    halves = {}
    for dx in (1, 0):
        halves[dx] = (send(G.at[slot(dx, FAR), pl.ds(0, gx2)], half_x.at[dx, 0], up),
                      send(G.at[slot(dx, FAR), pl.ds(gx2, gx2)], half_x.at[dx, 1], down))

    for copy in far_x:
        copy.wait_recv()
    forward(slot(0, FAR))
    pair_zp.wait_recv()
    forward(slot(1, PLUS))
    pair_zm.wait_recv()
    forward(slot(1, MINUS))

    for copy in y_back:
        copy.wait_recv()
    ld_mom.wait()

    @pl.loop(0, ROWS // 16)
    def _(r):
        at = pl.ds(pl.multiple_of(r * 16, 16), 16)
        delta = DL[at, :].astype(f32)
        moment = momentum_coef * M[at, :] + delta
        M[at, :] = moment
        GL[at, :] = GL[at, :] - outer_rate * (momentum_coef * moment + delta)

    st_mom = move(M, o_mom)
    st_glo = move(GL, o_glob)

    def add(s, lo, n, *terms):
        @pl.loop(0, n // 16)
        def _(r):
            at = pl.ds(pl.multiple_of(lo + r * 16, 16), 16)
            rows = pl.ds(pl.multiple_of(r * 16, 16), 16)
            total = G[s, at, :].astype(f32)
            for term in terms:
                total += term[rows, :].astype(f32)
            G[s, at, :] = total.astype(bf16)

    fulls = {}

    def x_full(dx):
        halves[dx][0].wait_recv()
        add(slot(dx, PLUS), 0, gx2, half_x.at[dx, 0])
        u = send(G.at[slot(dx, PLUS), gX], full_x.at[dx, 0], up)
        halves[dx][1].wait_recv()
        add(slot(dx, MINUS), gx2, gx2, half_x.at[dx, 1])
        d = send(G.at[slot(dx, MINUS), gX], full_x.at[dx, 1], down)
        fulls[dx] = (u, d)

    for copy in far_px:
        copy.wait_recv()
    pair_z2.wait_recv()
    x_full(1)
    x_parts[0].wait_recv()
    add(slot(0, FAR), RX, ROWS - RX, x_zpart.at[FAR])
    z_halves = (send(G.at[slot(0, FAR), pl.ds(RX, gz2)], half_z.at[0], up),
                send(G.at[slot(0, FAR), pl.ds(RX + gz2, gz2)], half_z.at[1], down))
    forward(slot(1, FAR))
    keys_swap = send(acc.at[pl.ds(TOK, TOK)], acc_in, core)
    x_full(0)

    x_parts[1].wait_recv()
    x_parts[2].wait_recv()
    add(slot(0, PLUS), RX, ROWS - RX, x_zpart.at[PLUS])
    add(slot(0, MINUS), RX, ROWS - RX, x_zpart.at[MINUS])
    z_halves[0].wait_recv()
    add(slot(0, PLUS), RX, gz2, half_z.at[0])
    u = send(G.at[slot(0, PLUS), gZ], full_z.at[0], up)
    z_halves[1].wait_recv()
    add(slot(0, MINUS), RX + gz2, gz2, half_z.at[1])
    z_fulls = (u, send(G.at[slot(0, MINUS), gZ], full_z.at[1], down))

    for copy in fulls[1]:
        copy.wait_recv()
    add(slot(1, ZERO), 0, RX, full_x.at[1, 0], full_x.at[1, 1])
    last = send(G.at[slot(1, ZERO), gX], x_last, pair)

    keys_swap.wait_recv()

    @pl.loop(0, TOK // 16)
    def _(r):
        at = pl.ds(pl.multiple_of(r * 16, 16), 16)
        keys_st[at, :] = ((acc[at, :] + acc_in[at, :]) * SCALE).astype(bf16)

    st_keys = move(keys_st, o_keys)

    def merge(lo, n, *terms):
        @pl.loop(0, n // 16)
        def _(r):
            at = pl.ds(pl.multiple_of(lo + r * 16, 16), 16)
            rows = pl.ds(pl.multiple_of(r * 16, 16), 16)
            grad = G[own, at, :].astype(f32)
            for term in terms:
                grad += term[rows, :].astype(f32)
            L[at, :] = mix_weight * (L[at, :] - inner_rate * grad) + (1.0 - mix_weight) * GL[at, :]

    for copy in fulls[0]:
        copy.wait_recv()
    last.wait_recv()
    merge(0, RX, full_x.at[0, 0], full_x.at[0, 1], x_last)
    st_x = move(L.at[gX], o_merged.at[gX])
    x_parts[3].wait_recv()
    for copy in z_fulls:
        copy.wait_recv()
    merge(RX, ROWS - RX, x_zpart.at[ZERO], full_z.at[0], full_z.at[1])
    st_z = move(L.at[gZ], o_merged.at[gZ])

    for n in (6, 7):
        mine, theirs = state["out"][n]
        mine.wait()
        theirs.wait_send()
    for n in range(8):
        state["out"][n][1].wait_recv()
    for copy in sent:
        copy.wait_send()
    for copy in (st_mom, st_glo, st_keys, st_x, st_z):
        copy.wait()


def shards(hidden, key_grad, local_weight, global_weight, momentum):
    bf16, f32 = jnp.bfloat16, jnp.float32
    vm = pltpu.VMEM
    anywhere = pl.BlockSpec(memory_space=pl.ANY)
    keys, back, merged, global_next, moment_next = pl.pallas_call(
        kernel,
        out_shape=(
            jax.ShapeDtypeStruct((TOK, KV), bf16),
            jax.ShapeDtypeStruct((TOK, D), bf16),
            jax.ShapeDtypeStruct((ROWS, KV), f32),
            jax.ShapeDtypeStruct((ROWS, KV), f32),
            jax.ShapeDtypeStruct((ROWS, KV), f32),
        ),
        in_specs=[anywhere] * 5,
        out_specs=[anywhere] * 5,
        scratch_shapes=[
            vm((8, ROWS, KV), bf16),
            vm((8, 2 * TOK, ROWS), bf16),
            vm((2 * TOK, KV), bf16),
            vm((8, ROWS, KV), bf16),
            vm((2 * TOK, KV), f32),
            vm((TOK, KV), f32),
            vm((TOK, KV), bf16),
            vm((2, 2 * TOK, ROWS), bf16),
            vm((ROWS, KV), f32),
            vm((ROWS, KV), f32),
            vm((ROWS, KV), f32),
            vm((ROWS, KV), bf16),
            vm((3, 128, KV), bf16),
            vm((128, KV), bf16),
            vm((128, KV), bf16),
            vm((ROWS, KV), bf16),
            vm((4, ROWS - RX, KV), bf16),
            vm((RX, KV), bf16),
            vm((2, 2, RX // 2, KV), bf16),
            vm((2, (ROWS - RX) // 2, KV), bf16),
            vm((2, 2, RX, KV), bf16),
            vm((2, ROWS - RX, KV), bf16),
            pltpu.SemaphoreType.DMA((64,)),
            pltpu.SemaphoreType.DMA((64,)),
            pltpu.SemaphoreType.DMA((32,)),
        ],
        compiler_params=pltpu.CompilerParams(
            collective_id=0, has_side_effects=True, vmem_limit_bytes=60 * 2**20
        ),
        cost_estimate=pl.CostEstimate(flops=3 * 2 * TOK * D * KV, bytes_accessed=26 * 2**20, transcendentals=0),
        name="step",
    )(hidden, key_grad, local_weight[0], global_weight, momentum)
    return (keys, back, merged[None], global_next, moment_next)


def solution(mesh):
    placed = (
        P(("worker", "fsdp"), None),
        P(("worker", "fsdp"), None),
        P("worker", "fsdp", None),
        P("fsdp", None),
        P("fsdp", None),
    )
    return jax.shard_map(
        shards,
        mesh=mesh,
        in_specs=placed,
        out_specs=(
            P(("worker", "fsdp"), None),
            P(("worker", "fsdp"), None),
            P("worker", "fsdp", None),
            P("fsdp", None),
            P("fsdp", None),
        ),
        check_vma=False,
    )
```

```python
import jax
import jax.numpy as jnp
from jax import lax
from jax.experimental import pallas as pl
from jax.experimental.pallas import tpu as pltpu
from jax.sharding import PartitionSpec as P

D = 8192
KV = 1024
TOK = 384
ROWS = 512
SCALE = D ** (-0.5)
MESH = pl.DeviceIdType.MESH

momentum_coef = 0.9
outer_rate = 0.7
inner_rate = 0.3
mix_weight = 0.5

AX = 320
RX = 288
ZERO, PLUS, MINUS, FAR = 0, 1, 2, 3


def slot(dx, dz):
    return dx * 4 + dz


def kernel(
    hid, kg, loc, glo, mom,
    o_keys, o_back, L, GL, M, g_own, x_own, x_last, full_own, full_z,
    W, H, K, G, acc, acc_in, back_st, DF, RY, A, RXH, DL,
    x_zpart, half_x, half_z, full_pair,
    ssem, rsem, lsem,
):
    f32, bf16 = jnp.float32, jnp.bfloat16
    w, f = lax.axis_index("worker"), lax.axis_index("fsdp")
    y, xh = w // 2, lax.rem(w, 2)
    xl, z, c = f // 8, lax.rem(f, 8) // 2, lax.rem(f, 2)

    def dev(y_, xh_, xl_, z_, c_):
        return (y_ * 2 + xh_, xl_ * 8 + z_ * 2 + c_)

    z_up, z_down = lax.rem(z + 1, 4), lax.rem(z + 3, 4)
    up, down = dev(y, xh, xl, z_up, c), dev(y, xh, xl, z_down, c)
    pair = dev(y, xh, 1 - xl, z, c)
    core = dev(y, xh, xl, z, 1 - c)
    cross = dev(y, 1 - xh, xl, z, c)
    ys = [dev(lax.rem(y + k, 4), xh, xl, z, c) for k in (1, 2, 3)]

    counts = {"remote": 0, "local": 0}
    sent = []

    def send(src, dst, to, keep=True):
        i = counts["remote"]
        counts["remote"] += 1
        copy = pltpu.make_async_remote_copy(
            src_ref=src, dst_ref=dst, send_sem=ssem.at[i], recv_sem=rsem.at[i],
            device_id=to, device_id_type=MESH,
        )
        copy.start()
        if keep:
            sent.append(copy)
        return copy

    def move(src, dst):
        i = counts["local"]
        counts["local"] += 1
        copy = pltpu.make_async_copy(src, dst, lsem.at[i])
        copy.start()
        return copy

    def columns(s, parity):
        dx, dz = divmod(s, 4)
        shift = (0, 1, 3, 2)[dz]
        chip = (xl + dx - 2 * xl * dx) * 4 + lax.rem(z + shift, 4)
        return pl.ds(pl.multiple_of((chip * 2 + parity) * ROWS, ROWS), ROWS)

    ld_loc = [move(loc.at[pl.ds(AX, ROWS - AX)], L.at[pl.ds(AX, ROWS - AX)]),
              move(loc.at[pl.ds(0, AX)], L.at[pl.ds(0, AX)])]
    ld_kg = move(kg, K.at[pl.ds(0, TOK)])
    ld_glo = move(glo, GL)
    order = [slot(1, FAR), slot(0, FAR), slot(1, PLUS), slot(1, MINUS),
             slot(0, PLUS), slot(0, MINUS), slot(1, ZERO), slot(0, ZERO)]

    barrier = pltpu.get_barrier_semaphore()
    partners = [up, down, pair, core, cross, *ys]
    for d in partners:
        pl.semaphore_signal(barrier, inc=1, device_id=d, device_id_type=MESH)
    pl.semaphore_wait(barrier, len(partners))

    def rounded(lo, n):
        @pl.loop(0, n // 32)
        def _(r):
            at = pl.ds(pl.multiple_of(lo + r * 32, 32), 32)
            W[slot(0, ZERO), at, :] = L[at, :].astype(bf16)

    aX, aZ = pl.ds(0, AX), pl.ds(AX, ROWS - AX)
    hX = (pl.ds(0, AX // 2), pl.ds(AX // 2, AX // 2))
    nz = (ROWS - AX) // 2
    hZ = (pl.ds(AX, nz), pl.ds(AX + nz, nz))
    own = slot(0, ZERO)

    def w_send(src, dst, rows, to):
        return send(W.at[src, rows], W.at[dst, rows], to)

    ld_loc[0].wait()
    rounded(AX, ROWS - AX)
    up_z = w_send(own, slot(0, MINUS), aZ, up)
    down_z = w_send(own, slot(0, PLUS), aZ, down)
    ld_loc[1].wait()
    rounded(0, AX)
    pair_x = w_send(own, slot(1, ZERO), aX, pair)
    up_x = w_send(own, slot(0, MINUS), aX, up)
    down_x = w_send(own, slot(0, PLUS), aX, down)
    pair_z = w_send(own, slot(1, ZERO), aZ, pair)

    sw_kg = send(kg, K.at[pl.ds(TOK, TOK)], core)
    sw_hid, ld_hid = {}, {}
    for s in order:
        sw_hid[s] = send(hid.at[:, columns(s, 1 - c)], H.at[s, pl.ds(TOK, TOK)], core)
        ld_hid[s] = move(hid.at[:, columns(s, c)], H.at[s, pl.ds(0, TOK)])
    ld_mom = move(mom, M)

    ld_glo.wait()

    @pl.loop(0, ROWS // 32)
    def _(r):
        at = pl.ds(pl.multiple_of(r * 32, 32), 32)
        DF[at, :] = GL[at, :] - L[at, :]

    def quarter(q):
        return pl.ds(pl.multiple_of(q * 128, 128), 128)

    y_parts = [send(DF.at[quarter(lax.rem(y + k, 4))], RY.at[k - 1], ys[k - 1]) for k in (1, 2, 3)]

    ld_kg.wait()
    sw_kg.wait_recv()

    def product(s):
        ld_hid[s].wait()
        sw_hid[s].wait_recv()

        @pl.loop(0, KV // 256)
        def _(j):
            at = pl.ds(pl.multiple_of(j * 256, 256), 256)
            term = lax.dot_general(H[s], K[:, at], (((0,), (0,)), ((), ())), preferred_element_type=f32)
            where = g_own if s == own else G.at[s]
            where[:, at] = (term * SCALE).astype(bf16)

    state = {"first": True, "n": 0, "out": {}}

    def forward(s):
        first = state["first"]
        state["first"] = False

        @pl.loop(0, KV // 256)
        def _(j):
            at = pl.ds(pl.multiple_of(j * 256, 256), 256)
            part = jnp.dot(H[s], W[s, :, at], preferred_element_type=f32)
            if first:
                acc[:, at] = part
            else:
                acc[:, at] += part

        n = state["n"]
        state["n"] += 1
        b = n % 2
        if n >= 2:
            state["out"][n - 2].wait_send()
        cols = columns(s, c)

        @pl.loop(0, ROWS // 256)
        def _(j):
            at = pl.ds(pl.multiple_of(j * 256, 256), 256)
            back = lax.dot_general(K[...], W[s, at, :], (((1,), (1,)), ((), ())), preferred_element_type=f32)
            back = (back * SCALE).astype(bf16)
            o_back[:, pl.ds(pl.multiple_of(cols.start + j * 256, 256), 256)] = back[:TOK]
            back_st[b, :, at] = back[TOK:]

        state["out"][n] = send(back_st.at[b], o_back.at[:, cols], core, keep=False)

    for s in order[:6]:
        product(s)
    up_z.wait_recv()
    down_z.wait_recv()
    far_z = (w_send(slot(0, MINUS), slot(0, FAR), hZ[0], up), w_send(slot(0, PLUS), slot(0, FAR), hZ[1], down))
    pair_zm = w_send(slot(0, MINUS), slot(1, MINUS), aZ, pair)
    pair_zp = w_send(slot(0, PLUS), slot(1, PLUS), aZ, pair)
    for s in order[6:]:
        product(s)
    pair_x.wait_recv()
    up_px = w_send(slot(1, ZERO), slot(1, MINUS), aX, up)
    down_px = w_send(slot(1, ZERO), slot(1, PLUS), aX, down)
    forward(own)

    for copy in y_parts:
        copy.wait_recv()

    @pl.loop(0, 128 // 32)
    def _(r):
        at = pl.ds(pl.multiple_of(r * 32, 32), 32)
        mine = DF[pl.ds(pl.multiple_of(y * 128 + r * 32, 32), 32), :]
        total = (mine + RY[0, at, :]) + (RY[1, at, :] + RY[2, at, :])
        A[at, :] = total.astype(bf16)

    x_sum = send(A, RXH, cross)

    up_x.wait_recv()
    down_x.wait_recv()
    far_x = (w_send(slot(0, MINUS), slot(0, FAR), hX[0], up), w_send(slot(0, PLUS), slot(0, FAR), hX[1], down))
    forward(slot(0, PLUS))
    forward(slot(0, MINUS))
    for copy in far_z:
        copy.wait_recv()
    pair_z2 = w_send(slot(0, FAR), slot(1, FAR), aZ, pair)
    pair_z.wait_recv()
    forward(slot(1, ZERO))

    x_sum.wait_recv()

    @pl.loop(0, 128 // 32)
    def _(r):
        at = pl.ds(pl.multiple_of(r * 32, 32), 32)
        total = A[at, :].astype(f32) + RXH[at, :].astype(f32)
        DL[pl.ds(pl.multiple_of(y * 128 + r * 32, 32), 32), :] = total * 0.125

    y_back = [send(DL.at[quarter(y)], DL.at[quarter(y)], ys[k - 1]) for k in (1, 2, 3)]

    up_px.wait_recv()
    down_px.wait_recv()
    far_px = (w_send(slot(1, MINUS), slot(1, FAR), hX[0], up), w_send(slot(1, PLUS), slot(1, FAR), hX[1], down))

    gX, gZ = pl.ds(0, RX), pl.ds(RX, ROWS - RX)
    gx2, gz2 = RX // 2, (ROWS - RX) // 2
    x_parts = [send(G.at[slot(1, dz), gZ], x_own if dz == ZERO else x_zpart.at[dz - 1], pair)
               for dz in (FAR, PLUS, MINUS, ZERO)]
    halves = {}
    for dx in (1, 0):
        halves[dx] = (send(G.at[slot(dx, FAR), pl.ds(0, gx2)], half_x.at[dx, 0], up),
                      send(G.at[slot(dx, FAR), pl.ds(gx2, gx2)], half_x.at[dx, 1], down))

    for copy in far_x:
        copy.wait_recv()
    forward(slot(0, FAR))
    pair_zp.wait_recv()
    forward(slot(1, PLUS))
    pair_zm.wait_recv()
    forward(slot(1, MINUS))

    for copy in y_back:
        copy.wait_recv()
    ld_mom.wait()

    @pl.loop(0, ROWS // 16)
    def _(r):
        at = pl.ds(pl.multiple_of(r * 16, 16), 16)
        delta = DL[at, :]
        moment = momentum_coef * M[at, :] + delta
        M[at, :] = moment
        GL[at, :] = GL[at, :] - outer_rate * (momentum_coef * moment + delta)

    def add(s, lo, n, *terms):
        @pl.loop(0, n // 16)
        def _(r):
            at = pl.ds(pl.multiple_of(lo + r * 16, 16), 16)
            rows = pl.ds(pl.multiple_of(r * 16, 16), 16)
            total = G[s, at, :].astype(f32)
            for term in terms:
                total += term[rows, :].astype(f32)
            G[s, at, :] = total.astype(bf16)

    fulls = {}

    def x_full(dx):
        halves[dx][0].wait_recv()
        add(slot(dx, PLUS), 0, gx2, half_x.at[dx, 0])
        full = full_pair if dx else full_own
        u = send(G.at[slot(dx, PLUS), gX], full.at[0], up)
        halves[dx][1].wait_recv()
        add(slot(dx, MINUS), gx2, gx2, half_x.at[dx, 1])
        d = send(G.at[slot(dx, MINUS), gX], full.at[1], down)
        fulls[dx] = (u, d)

    for copy in far_px:
        copy.wait_recv()
    pair_z2.wait_recv()
    x_full(1)
    x_parts[0].wait_recv()
    add(slot(0, FAR), RX, ROWS - RX, x_zpart.at[FAR - 1])
    z_halves = (send(G.at[slot(0, FAR), pl.ds(RX, gz2)], half_z.at[0], up),
                send(G.at[slot(0, FAR), pl.ds(RX + gz2, gz2)], half_z.at[1], down))
    forward(slot(1, FAR))
    keys_swap = send(acc.at[pl.ds(TOK, TOK)], acc_in, core)
    x_full(0)

    x_parts[1].wait_recv()
    x_parts[2].wait_recv()
    add(slot(0, PLUS), RX, ROWS - RX, x_zpart.at[PLUS - 1])
    add(slot(0, MINUS), RX, ROWS - RX, x_zpart.at[MINUS - 1])
    z_halves[0].wait_recv()
    add(slot(0, PLUS), RX, gz2, half_z.at[0])
    u = send(G.at[slot(0, PLUS), gZ], full_z.at[0], up)
    z_halves[1].wait_recv()
    add(slot(0, MINUS), RX + gz2, gz2, half_z.at[1])
    z_fulls = (u, send(G.at[slot(0, MINUS), gZ], full_z.at[1], down))

    for copy in fulls[1]:
        copy.wait_recv()
    add(slot(1, ZERO), 0, RX, full_pair.at[0], full_pair.at[1])
    last = send(G.at[slot(1, ZERO), gX], x_last, pair)

    keys_swap.wait_recv()

    @pl.loop(0, TOK // 16)
    def _(r):
        at = pl.ds(pl.multiple_of(r * 16, 16), 16)
        o_keys[at, :] = ((acc[at, :] + acc_in[at, :]) * SCALE).astype(bf16)

    for copy in fulls[0]:
        copy.wait_recv()
    last.wait_recv()
    x_parts[3].wait_recv()
    for copy in z_fulls:
        copy.wait_recv()
    for n in (6, 7):
        state["out"][n].wait_send()
    for n in range(8):
        state["out"][n].wait_recv()
    for copy in sent:
        copy.wait_send()


def finish(
    keys, back, L, GL, M, g_own, x_own, x_last, full_own, full_z,
    o_keys, o_back, o_merged, o_glob, o_mom, merged, sem,
):
    f32 = jnp.float32
    copies = []

    def move(src, dst):
        copy = pltpu.make_async_copy(src, dst, sem.at[len(copies)])
        copy.start()
        copies.append(copy)

    def merge(lo, n, *terms):
        @pl.loop(0, n // 16)
        def _(r):
            at = pl.ds(pl.multiple_of(lo + r * 16, 16), 16)
            rows = pl.ds(pl.multiple_of(r * 16, 16), 16)
            grad = g_own[at, :].astype(f32)
            for term in terms:
                grad += term[rows, :].astype(f32)
            merged[at, :] = mix_weight * (L[at, :] - inner_rate * grad) + (1.0 - mix_weight) * GL[at, :]

        move(merged.at[pl.ds(lo, n)], o_merged.at[pl.ds(lo, n)])

    move(back, o_back)
    move(M, o_mom)
    move(GL, o_glob)
    move(keys, o_keys)
    merge(0, RX, full_own.at[0], full_own.at[1], x_last)
    merge(RX, ROWS - RX, x_own, full_z.at[0], full_z.at[1])
    for copy in copies:
        copy.wait()


def shards(hidden, key_grad, local_weight, global_weight, momentum):
    bf16, f32 = jnp.bfloat16, jnp.float32
    vm = pltpu.VMEM
    anywhere = pl.BlockSpec(memory_space=pl.ANY)
    inside = pl.BlockSpec(memory_space=pltpu.VMEM)
    held = [
        vm((TOK, KV), bf16),
        vm((TOK, D), bf16),
        vm((ROWS, KV), f32),
        vm((ROWS, KV), f32),
        vm((ROWS, KV), f32),
        vm((ROWS, KV), bf16),
        vm((ROWS - RX, KV), bf16),
        vm((RX, KV), bf16),
        vm((2, RX, KV), bf16),
        vm((2, ROWS - RX, KV), bf16),
    ]
    parts = pl.pallas_call(
        kernel,
        out_shape=held,
        in_specs=[anywhere] * 5,
        out_specs=[inside] * len(held),
        scratch_shapes=[
            vm((8, ROWS, KV), bf16),
            vm((8, 2 * TOK, ROWS), bf16),
            vm((2 * TOK, KV), bf16),
            vm((8, ROWS, KV), bf16),
            vm((2 * TOK, KV), f32),
            vm((TOK, KV), f32),
            vm((2, TOK, ROWS), bf16),
            vm((ROWS, KV), f32),
            vm((3, 128, KV), f32),
            vm((128, KV), bf16),
            vm((128, KV), bf16),
            vm((ROWS, KV), f32),
            vm((3, ROWS - RX, KV), bf16),
            vm((2, 2, RX // 2, KV), bf16),
            vm((2, (ROWS - RX) // 2, KV), bf16),
            vm((2, RX, KV), bf16),
            pltpu.SemaphoreType.DMA((64,)),
            pltpu.SemaphoreType.DMA((64,)),
            pltpu.SemaphoreType.DMA((32,)),
        ],
        compiler_params=pltpu.CompilerParams(
            collective_id=0, has_side_effects=True, vmem_limit_bytes=44 * 2**20
        ),
        cost_estimate=pl.CostEstimate(flops=3 * 2 * TOK * D * KV, bytes_accessed=26 * 2**20, transcendentals=0),
        name="step",
    )(hidden, key_grad, local_weight[0], global_weight, momentum)
    parts = [pltpu.with_memory_space_constraint(a, pltpu.VMEM) for a in parts]
    keys, back, merged, global_next, moment_next = pl.pallas_call(
        finish,
        out_shape=(
            jax.ShapeDtypeStruct((TOK, KV), bf16),
            jax.ShapeDtypeStruct((TOK, D), bf16),
            jax.ShapeDtypeStruct((ROWS, KV), f32),
            jax.ShapeDtypeStruct((ROWS, KV), f32),
            jax.ShapeDtypeStruct((ROWS, KV), f32),
        ),
        in_specs=[inside] * len(held),
        out_specs=[anywhere] * 5,
        scratch_shapes=[vm((ROWS, KV), f32), pltpu.SemaphoreType.DMA((8,))],
        compiler_params=pltpu.CompilerParams(vmem_limit_bytes=8 * 2**20),
        name="finish",
    )(*parts)
    return (keys, back, merged[None], global_next, moment_next)


def solution(mesh):
    placed = (
        P(("worker", "fsdp"), None),
        P(("worker", "fsdp"), None),
        P("worker", "fsdp", None),
        P("fsdp", None),
        P("fsdp", None),
    )
    return jax.shard_map(
        shards,
        mesh=mesh,
        in_specs=placed,
        out_specs=(
            P(("worker", "fsdp"), None),
            P(("worker", "fsdp"), None),
            P("worker", "fsdp", None),
            P("fsdp", None),
            P("fsdp", None),
        ),
        check_vma=False,
    )
```

```python
import jax
import jax.numpy as jnp
from jax import lax
from jax.experimental import pallas as pl
from jax.experimental.pallas import tpu as pltpu
from jax.sharding import PartitionSpec as P

D = 8192
KV = 1024
TOK = 384
ROWS = 512
SCALE = D ** (-0.5)
MESH = pl.DeviceIdType.MESH

momentum_coef = 0.9
outer_rate = 0.7
inner_rate = 0.3
mix_weight = 0.5

AX = 304
RX = 288
ZERO, PLUS, MINUS, FAR = 0, 1, 2, 3


def slot(dx, dz):
    return dx * 4 + dz


def kernel(
    hid, kg, loc, glo, mom,
    o_keys, o_back, L, GL, M, g_own, x_own, x_last, full_own, full_z,
    W, H, K, G, acc, acc_in, back_st, DF, RY, A, RXH, DL,
    x_zpart, half_x, half_z, full_pair,
    ssem, rsem, lsem,
):
    f32, bf16 = jnp.float32, jnp.bfloat16
    w, f = lax.axis_index("worker"), lax.axis_index("fsdp")
    y, xh = w // 2, lax.rem(w, 2)
    xl, z, c = f // 8, lax.rem(f, 8) // 2, lax.rem(f, 2)

    def dev(y_, xh_, xl_, z_, c_):
        return (y_ * 2 + xh_, xl_ * 8 + z_ * 2 + c_)

    z_up, z_down = lax.rem(z + 1, 4), lax.rem(z + 3, 4)
    up, down = dev(y, xh, xl, z_up, c), dev(y, xh, xl, z_down, c)
    pair = dev(y, xh, 1 - xl, z, c)
    core = dev(y, xh, xl, z, 1 - c)
    cross = dev(y, 1 - xh, xl, z, c)
    ys = [dev(lax.rem(y + k, 4), xh, xl, z, c) for k in (1, 2, 3)]

    counts = {"remote": 0, "local": 0}
    sent = []

    def send(src, dst, to, keep=True):
        i = counts["remote"]
        counts["remote"] += 1
        copy = pltpu.make_async_remote_copy(
            src_ref=src, dst_ref=dst, send_sem=ssem.at[i], recv_sem=rsem.at[i],
            device_id=to, device_id_type=MESH,
        )
        copy.start()
        if keep:
            sent.append(copy)
        return copy

    def move(src, dst):
        i = counts["local"]
        counts["local"] += 1
        copy = pltpu.make_async_copy(src, dst, lsem.at[i])
        copy.start()
        return copy

    def columns(s, parity):
        dx, dz = divmod(s, 4)
        shift = (0, 1, 3, 2)[dz]
        chip = (xl + dx - 2 * xl * dx) * 4 + lax.rem(z + shift, 4)
        return pl.ds(pl.multiple_of((chip * 2 + parity) * ROWS, ROWS), ROWS)

    ld_loc = [move(loc.at[pl.ds(AX, ROWS - AX)], L.at[pl.ds(AX, ROWS - AX)]),
              move(loc.at[pl.ds(0, AX)], L.at[pl.ds(0, AX)])]
    ld_kg = move(kg, K.at[pl.ds(0, TOK)])
    ld_glo = move(glo, GL)
    order = [slot(1, FAR), slot(0, FAR), slot(1, PLUS), slot(1, MINUS),
             slot(0, PLUS), slot(0, MINUS), slot(1, ZERO), slot(0, ZERO)]

    barrier = pltpu.get_barrier_semaphore()
    partners = [up, down, pair, core, cross, *ys]
    for d in partners:
        pl.semaphore_signal(barrier, inc=1, device_id=d, device_id_type=MESH)
    pl.semaphore_wait(barrier, len(partners))

    def rounded(lo, n):
        @pl.loop(0, n // 16)
        def _(r):
            at = pl.ds(pl.multiple_of(lo + r * 16, 16), 16)
            W[slot(0, ZERO), at, :] = L[at, :].astype(bf16)

    aX, aZ = pl.ds(0, AX), pl.ds(AX, ROWS - AX)
    ax2 = (AX // 32) * 16
    hX = (pl.ds(0, ax2), pl.ds(ax2, AX - ax2))
    hPX = (pl.ds(0, AX - ax2), pl.ds(AX - ax2, ax2))
    az2 = (ROWS - AX) // 32 * 16
    hZ = (pl.ds(AX, az2), pl.ds(AX + az2, ROWS - AX - az2))
    own = slot(0, ZERO)

    def w_send(src, dst, rows, to):
        return send(W.at[src, rows], W.at[dst, rows], to)

    ld_loc[0].wait()
    rounded(AX, ROWS - AX)
    up_z = w_send(own, slot(0, MINUS), aZ, up)
    down_z = w_send(own, slot(0, PLUS), aZ, down)
    ld_loc[1].wait()
    rounded(0, AX)
    pair_x = w_send(own, slot(1, ZERO), aX, pair)
    up_x = w_send(own, slot(0, MINUS), aX, up)
    down_x = w_send(own, slot(0, PLUS), aX, down)
    pair_z = w_send(own, slot(1, ZERO), aZ, pair)

    sw_kg = send(kg, K.at[pl.ds(TOK, TOK)], core)
    sw_hid, ld_hid = {}, {}
    for s in order:
        sw_hid[s] = send(hid.at[:, columns(s, 1 - c)], H.at[s, pl.ds(TOK, TOK)], core)
        ld_hid[s] = move(hid.at[:, columns(s, c)], H.at[s, pl.ds(0, TOK)])
    ld_mom = move(mom, M)

    ld_glo.wait()

    @pl.loop(0, ROWS // 32)
    def _(r):
        at = pl.ds(pl.multiple_of(r * 32, 32), 32)
        DF[at, :] = GL[at, :] - L[at, :]

    def quarter(q):
        return pl.ds(pl.multiple_of(q * 128, 128), 128)

    y_parts = [send(DF.at[quarter(lax.rem(y + k, 4))], RY.at[k - 1], ys[k - 1]) for k in (1, 2, 3)]

    ld_kg.wait()
    sw_kg.wait_recv()

    def product(s):
        ld_hid[s].wait()
        sw_hid[s].wait_recv()

        @pl.loop(0, KV // 256)
        def _(j):
            at = pl.ds(pl.multiple_of(j * 256, 256), 256)
            term = lax.dot_general(H[s], K[:, at], (((0,), (0,)), ((), ())), preferred_element_type=f32)
            where = g_own if s == own else G.at[s]
            where[:, at] = (term * SCALE).astype(bf16)

    state = {"first": True, "n": 0, "out": {}}

    def forward(s):
        first = state["first"]
        state["first"] = False

        @pl.loop(0, KV // 256)
        def _(j):
            at = pl.ds(pl.multiple_of(j * 256, 256), 256)
            part = jnp.dot(H[s], W[s, :, at], preferred_element_type=f32)
            if first:
                acc[:, at] = part
            else:
                acc[:, at] += part

        n = state["n"]
        state["n"] += 1
        b = n % 2
        if n >= 2:
            state["out"][n - 2].wait_send()
        cols = columns(s, c)

        @pl.loop(0, ROWS // 256)
        def _(j):
            at = pl.ds(pl.multiple_of(j * 256, 256), 256)
            back = lax.dot_general(K[...], W[s, at, :], (((1,), (1,)), ((), ())), preferred_element_type=f32)
            back = (back * SCALE).astype(bf16)
            o_back[:, pl.ds(pl.multiple_of(cols.start + j * 256, 256), 256)] = back[:TOK]
            back_st[b, :, at] = back[TOK:]

        state["out"][n] = send(back_st.at[b], o_back.at[:, cols], core, keep=False)

    for s in order[:6]:
        product(s)
    up_z.wait_recv()
    down_z.wait_recv()
    far_z = (w_send(slot(0, MINUS), slot(0, FAR), hZ[0], up), w_send(slot(0, PLUS), slot(0, FAR), hZ[1], down))
    pair_zm = w_send(slot(0, MINUS), slot(1, MINUS), aZ, pair)
    pair_zp = w_send(slot(0, PLUS), slot(1, PLUS), aZ, pair)
    for s in order[6:]:
        product(s)
    pair_x.wait_recv()
    up_px = w_send(slot(1, ZERO), slot(1, MINUS), aX, up)
    down_px = w_send(slot(1, ZERO), slot(1, PLUS), aX, down)
    forward(own)

    up_x.wait_recv()
    down_x.wait_recv()
    far_x = (w_send(slot(0, MINUS), slot(0, FAR), hX[0], up), w_send(slot(0, PLUS), slot(0, FAR), hX[1], down))
    for copy in y_parts:
        copy.wait_recv()

    @pl.loop(0, 128 // 32)
    def _(r):
        at = pl.ds(pl.multiple_of(r * 32, 32), 32)
        mine = DF[pl.ds(pl.multiple_of(y * 128 + r * 32, 32), 32), :]
        total = (mine + RY[0, at, :]) + (RY[1, at, :] + RY[2, at, :])
        A[at, :] = total.astype(bf16)

    x_sum = send(A, RXH, cross)

    forward(slot(0, PLUS))
    forward(slot(0, MINUS))
    for copy in far_z:
        copy.wait_recv()
    pair_z2 = w_send(slot(0, FAR), slot(1, FAR), aZ, pair)
    pair_z.wait_recv()
    forward(slot(1, ZERO))

    up_px.wait_recv()
    down_px.wait_recv()
    far_px = (w_send(slot(1, MINUS), slot(1, FAR), hPX[0], up), w_send(slot(1, PLUS), slot(1, FAR), hPX[1], down))

    gX, gZ = pl.ds(0, RX), pl.ds(RX, ROWS - RX)
    gx2, gz2 = RX // 2, (ROWS - RX) // 2
    x_parts = [send(G.at[slot(1, dz), gZ], x_own if dz == ZERO else x_zpart.at[dz - 1], pair)
               for dz in (FAR, PLUS, MINUS, ZERO)]
    halves = {}
    for dx in (1, 0):
        halves[dx] = (send(G.at[slot(dx, FAR), pl.ds(0, gx2)], half_x.at[dx, 0], up),
                      send(G.at[slot(dx, FAR), pl.ds(gx2, gx2)], half_x.at[dx, 1], down))

    def add(s, lo, n, *terms):
        @pl.loop(0, n // 16)
        def _(r):
            at = pl.ds(pl.multiple_of(lo + r * 16, 16), 16)
            rows = pl.ds(pl.multiple_of(r * 16, 16), 16)
            total = G[s, at, :].astype(f32)
            for term in terms:
                total += term[rows, :].astype(f32)
            G[s, at, :] = total.astype(bf16)

    fulls = {}

    def x_full(dx):
        halves[dx][0].wait_recv()
        add(slot(dx, PLUS), 0, gx2, half_x.at[dx, 0])
        full = full_pair if dx else full_own
        u = send(G.at[slot(dx, PLUS), gX], full.at[0], up)
        halves[dx][1].wait_recv()
        add(slot(dx, MINUS), gx2, gx2, half_x.at[dx, 1])
        d = send(G.at[slot(dx, MINUS), gX], full.at[1], down)
        fulls[dx] = (u, d)

    for copy in far_x:
        copy.wait_recv()
    forward(slot(0, FAR))
    pair_zm.wait_recv()
    forward(slot(1, MINUS))
    x_sum.wait_recv()

    @pl.loop(0, 128 // 32)
    def _(r):
        at = pl.ds(pl.multiple_of(r * 32, 32), 32)
        total = A[at, :].astype(f32) + RXH[at, :].astype(f32)
        DL[pl.ds(pl.multiple_of(y * 128 + r * 32, 32), 32), :] = total * 0.125

    y_back = [send(DL.at[quarter(y)], DL.at[quarter(y)], ys[k - 1]) for k in (1, 2, 3)]

    pair_zp.wait_recv()
    forward(slot(1, PLUS))
    for copy in far_px:
        copy.wait_recv()
    pair_z2.wait_recv()
    forward(slot(1, FAR))
    keys_swap = send(acc.at[pl.ds(TOK, TOK)], acc_in, core)
    x_full(1)
    x_parts[0].wait_recv()
    add(slot(0, FAR), RX, ROWS - RX, x_zpart.at[FAR - 1])
    z_halves = (send(G.at[slot(0, FAR), pl.ds(RX, gz2)], half_z.at[0], up),
                send(G.at[slot(0, FAR), pl.ds(RX + gz2, gz2)], half_z.at[1], down))
    x_full(0)

    keys_swap.wait_recv()

    @pl.loop(0, TOK // 16)
    def _(r):
        at = pl.ds(pl.multiple_of(r * 16, 16), 16)
        o_keys[at, :] = ((acc[at, :] + acc_in[at, :]) * SCALE).astype(bf16)

    for copy in y_back:
        copy.wait_recv()
    ld_mom.wait()

    @pl.loop(0, ROWS // 16)
    def _(r):
        at = pl.ds(pl.multiple_of(r * 16, 16), 16)
        delta = DL[at, :]
        moment = momentum_coef * M[at, :] + delta
        M[at, :] = moment
        GL[at, :] = GL[at, :] - outer_rate * (momentum_coef * moment + delta)

    x_parts[1].wait_recv()
    x_parts[2].wait_recv()
    add(slot(0, PLUS), RX, ROWS - RX, x_zpart.at[PLUS - 1])
    add(slot(0, MINUS), RX, ROWS - RX, x_zpart.at[MINUS - 1])
    z_halves[0].wait_recv()
    add(slot(0, PLUS), RX, gz2, half_z.at[0])
    u = send(G.at[slot(0, PLUS), gZ], full_z.at[0], up)
    z_halves[1].wait_recv()
    add(slot(0, MINUS), RX + gz2, gz2, half_z.at[1])
    z_fulls = (u, send(G.at[slot(0, MINUS), gZ], full_z.at[1], down))

    for copy in fulls[1]:
        copy.wait_recv()
    add(slot(1, ZERO), 0, RX, full_pair.at[0], full_pair.at[1])
    last = send(G.at[slot(1, ZERO), gX], x_last, pair)

    for copy in fulls[0]:
        copy.wait_recv()
    last.wait_recv()
    x_parts[3].wait_recv()
    for copy in z_fulls:
        copy.wait_recv()
    for n in (6, 7):
        state["out"][n].wait_send()
    for n in range(8):
        state["out"][n].wait_recv()
    for copy in sent:
        copy.wait_send()


def finish(
    keys, back, L, GL, M, g_own, x_own, x_last, full_own, full_z,
    o_keys, o_back, o_merged, o_glob, o_mom, merged, sem,
):
    f32 = jnp.float32
    copies = []

    def move(src, dst):
        copy = pltpu.make_async_copy(src, dst, sem.at[len(copies)])
        copy.start()
        copies.append(copy)

    def merge(lo, n, *terms):
        @pl.loop(0, n // 16)
        def _(r):
            at = pl.ds(pl.multiple_of(lo + r * 16, 16), 16)
            rows = pl.ds(pl.multiple_of(r * 16, 16), 16)
            grad = g_own[at, :].astype(f32)
            for term in terms:
                grad += term[rows, :].astype(f32)
            merged[at, :] = mix_weight * (L[at, :] - inner_rate * grad) + (1.0 - mix_weight) * GL[at, :]

        move(merged.at[pl.ds(lo, n)], o_merged.at[pl.ds(lo, n)])

    move(back, o_back)
    move(M, o_mom)
    move(GL, o_glob)
    move(keys, o_keys)
    merge(0, RX, full_own.at[0], full_own.at[1], x_last)
    merge(RX, ROWS - RX, x_own, full_z.at[0], full_z.at[1])
    for copy in copies:
        copy.wait()


def shards(hidden, key_grad, local_weight, global_weight, momentum):
    bf16, f32 = jnp.bfloat16, jnp.float32
    vm = pltpu.VMEM
    anywhere = pl.BlockSpec(memory_space=pl.ANY)
    inside = pl.BlockSpec(memory_space=pltpu.VMEM)
    held = [
        vm((TOK, KV), bf16),
        vm((TOK, D), bf16),
        vm((ROWS, KV), f32),
        vm((ROWS, KV), f32),
        vm((ROWS, KV), f32),
        vm((ROWS, KV), bf16),
        vm((ROWS - RX, KV), bf16),
        vm((RX, KV), bf16),
        vm((2, RX, KV), bf16),
        vm((2, ROWS - RX, KV), bf16),
    ]
    parts = pl.pallas_call(
        kernel,
        out_shape=held,
        in_specs=[anywhere] * 5,
        out_specs=[inside] * len(held),
        scratch_shapes=[
            vm((8, ROWS, KV), bf16),
            vm((8, 2 * TOK, ROWS), bf16),
            vm((2 * TOK, KV), bf16),
            vm((8, ROWS, KV), bf16),
            vm((2 * TOK, KV), f32),
            vm((TOK, KV), f32),
            vm((2, TOK, ROWS), bf16),
            vm((ROWS, KV), f32),
            vm((3, 128, KV), f32),
            vm((128, KV), bf16),
            vm((128, KV), bf16),
            vm((ROWS, KV), f32),
            vm((3, ROWS - RX, KV), bf16),
            vm((2, 2, RX // 2, KV), bf16),
            vm((2, (ROWS - RX) // 2, KV), bf16),
            vm((2, RX, KV), bf16),
            pltpu.SemaphoreType.DMA((64,)),
            pltpu.SemaphoreType.DMA((64,)),
            pltpu.SemaphoreType.DMA((32,)),
        ],
        compiler_params=pltpu.CompilerParams(
            collective_id=0, has_side_effects=True, vmem_limit_bytes=44 * 2**20
        ),
        cost_estimate=pl.CostEstimate(flops=3 * 2 * TOK * D * KV, bytes_accessed=26 * 2**20, transcendentals=0),
        name="step",
    )(hidden, key_grad, local_weight[0], global_weight, momentum)
    parts = [pltpu.with_memory_space_constraint(a, pltpu.VMEM) for a in parts]
    keys, back, merged, global_next, moment_next = pl.pallas_call(
        finish,
        out_shape=(
            jax.ShapeDtypeStruct((TOK, KV), bf16),
            jax.ShapeDtypeStruct((TOK, D), bf16),
            jax.ShapeDtypeStruct((ROWS, KV), f32),
            jax.ShapeDtypeStruct((ROWS, KV), f32),
            jax.ShapeDtypeStruct((ROWS, KV), f32),
        ),
        in_specs=[inside] * len(held),
        out_specs=[anywhere] * 5,
        scratch_shapes=[vm((ROWS, KV), f32), pltpu.SemaphoreType.DMA((8,))],
        compiler_params=pltpu.CompilerParams(vmem_limit_bytes=8 * 2**20),
        name="finish",
    )(*parts)
    return (keys, back, merged[None], global_next, moment_next)


def solution(mesh):
    placed = (
        P(("worker", "fsdp"), None),
        P(("worker", "fsdp"), None),
        P("worker", "fsdp", None),
        P("fsdp", None),
        P("fsdp", None),
    )
    return jax.shard_map(
        shards,
        mesh=mesh,
        in_specs=placed,
        out_specs=(
            P(("worker", "fsdp"), None),
            P(("worker", "fsdp"), None),
            P("worker", "fsdp", None),
            P("fsdp", None),
            P("fsdp", None),
        ),
        check_vma=False,
    )
```

```python
import jax
import jax.numpy as jnp
from jax import lax
from jax.experimental import pallas as pl
from jax.experimental.pallas import tpu as pltpu
from jax.sharding import PartitionSpec as P

D = 8192
KV = 1024
TOK = 384
ROWS = 512
SCALE = D ** (-0.5)
MESH = pl.DeviceIdType.MESH

momentum_coef = 0.9
outer_rate = 0.7
inner_rate = 0.3
mix_weight = 0.5

AX = 320
RX = 288
ZERO, PLUS, MINUS, FAR = 0, 1, 2, 3


def slot(dx, dz):
    return dx * 4 + dz


def kernel(
    hid, kg, loc, glo, mom,
    o_keys, o_back, L, GL, M, g_own, x_own, x_last, full_own, full_z,
    W, H, K, G, acc, acc_in, back_st, DF, RY, A, RXH, DL,
    x_zpart, half_x, half_z, full_pair,
    ssem, rsem, lsem,
):
    f32, bf16 = jnp.float32, jnp.bfloat16
    w, f = lax.axis_index("worker"), lax.axis_index("fsdp")
    y, xh = w // 2, lax.rem(w, 2)
    xl, z, c = f // 8, lax.rem(f, 8) // 2, lax.rem(f, 2)

    def dev(y_, xh_, xl_, z_, c_):
        return (y_ * 2 + xh_, xl_ * 8 + z_ * 2 + c_)

    z_up, z_down = lax.rem(z + 1, 4), lax.rem(z + 3, 4)
    up, down = dev(y, xh, xl, z_up, c), dev(y, xh, xl, z_down, c)
    pair = dev(y, xh, 1 - xl, z, c)
    core = dev(y, xh, xl, z, 1 - c)
    cross = dev(y, 1 - xh, xl, z, c)
    ys = [dev(lax.rem(y + k, 4), xh, xl, z, c) for k in (1, 2, 3)]

    counts = {"remote": 0, "local": 0}
    sent = []

    def send(src, dst, to, keep=True):
        i = counts["remote"]
        counts["remote"] += 1
        copy = pltpu.make_async_remote_copy(
            src_ref=src, dst_ref=dst, send_sem=ssem.at[i], recv_sem=rsem.at[i],
            device_id=to, device_id_type=MESH,
        )
        copy.start()
        if keep:
            sent.append(copy)
        return copy

    def move(src, dst):
        i = counts["local"]
        counts["local"] += 1
        copy = pltpu.make_async_copy(src, dst, lsem.at[i])
        copy.start()
        return copy

    def columns(s, parity):
        dx, dz = divmod(s, 4)
        shift = (0, 1, 3, 2)[dz]
        chip = (xl + dx - 2 * xl * dx) * 4 + lax.rem(z + shift, 4)
        return pl.ds(pl.multiple_of((chip * 2 + parity) * ROWS, ROWS), ROWS)

    ld_loc = [move(loc.at[pl.ds(AX, ROWS - AX)], L.at[pl.ds(AX, ROWS - AX)]),
              move(loc.at[pl.ds(0, AX)], L.at[pl.ds(0, AX)])]
    ld_kg = move(kg, K.at[pl.ds(0, TOK)])
    ld_glo = move(glo, GL)
    order = [slot(1, FAR), slot(0, FAR), slot(1, PLUS), slot(1, MINUS),
             slot(0, PLUS), slot(0, MINUS), slot(1, ZERO), slot(0, ZERO)]

    barrier = pltpu.get_barrier_semaphore()
    partners = [up, down, pair, core, cross, *ys]
    for d in partners:
        pl.semaphore_signal(barrier, inc=1, device_id=d, device_id_type=MESH)
    pl.semaphore_wait(barrier, len(partners))

    def rounded(lo, n):
        @pl.loop(0, n // 16)
        def _(r):
            at = pl.ds(pl.multiple_of(lo + r * 16, 16), 16)
            W[slot(0, ZERO), at, :] = L[at, :].astype(bf16)

    aX, aZ = pl.ds(0, AX), pl.ds(AX, ROWS - AX)
    ax2 = (AX // 32) * 16
    hX = (pl.ds(0, ax2), pl.ds(ax2, AX - ax2))
    hPX = (pl.ds(0, AX - ax2), pl.ds(AX - ax2, ax2))
    az2 = (ROWS - AX) // 32 * 16
    hZ = (pl.ds(AX, az2), pl.ds(AX + az2, ROWS - AX - az2))
    own = slot(0, ZERO)

    def w_send(src, dst, rows, to):
        return send(W.at[src, rows], W.at[dst, rows], to)

    ld_loc[0].wait()
    rounded(AX, ROWS - AX)
    up_z = w_send(own, slot(0, MINUS), aZ, up)
    down_z = w_send(own, slot(0, PLUS), aZ, down)
    ld_loc[1].wait()
    rounded(0, AX)
    pair_x = w_send(own, slot(1, ZERO), aX, pair)
    up_x = w_send(own, slot(0, MINUS), aX, up)
    down_x = w_send(own, slot(0, PLUS), aX, down)
    pair_z = w_send(own, slot(1, ZERO), aZ, pair)

    sw_kg = send(kg, K.at[pl.ds(TOK, TOK)], core)
    sw_hid, ld_hid = {}, {}
    for s in order:
        sw_hid[s] = send(hid.at[:, columns(s, 1 - c)], H.at[s, pl.ds(TOK, TOK)], core)
        ld_hid[s] = move(hid.at[:, columns(s, c)], H.at[s, pl.ds(0, TOK)])
    ld_mom = move(mom, M)

    ld_glo.wait()

    @pl.loop(0, ROWS // 32)
    def _(r):
        at = pl.ds(pl.multiple_of(r * 32, 32), 32)
        DF[at, :] = GL[at, :] - L[at, :]

    def quarter(q):
        return pl.ds(pl.multiple_of(q * 128, 128), 128)

    y_parts = [send(DF.at[quarter(lax.rem(y + k, 4))], RY.at[k - 1], ys[k - 1]) for k in (1, 2, 3)]

    ld_kg.wait()
    sw_kg.wait_recv()

    def product(s):
        ld_hid[s].wait()
        sw_hid[s].wait_recv()

        @pl.loop(0, KV // 256)
        def _(j):
            at = pl.ds(pl.multiple_of(j * 256, 256), 256)
            term = lax.dot_general(H[s], K[:, at], (((0,), (0,)), ((), ())), preferred_element_type=f32)
            where = g_own if s == own else G.at[s]
            where[:, at] = (term * SCALE).astype(bf16)

    state = {"first": True, "n": 0, "out": {}}

    def forward(s):
        first = state["first"]
        state["first"] = False

        @pl.loop(0, KV // 256)
        def _(j):
            at = pl.ds(pl.multiple_of(j * 256, 256), 256)
            part = jnp.dot(H[s], W[s, :, at], preferred_element_type=f32)
            if first:
                acc[:, at] = part
            else:
                acc[:, at] += part

        n = state["n"]
        state["n"] += 1
        b = n % 2
        if n >= 2:
            state["out"][n - 2].wait_send()
        cols = columns(s, c)

        @pl.loop(0, ROWS // 256)
        def _(j):
            at = pl.ds(pl.multiple_of(j * 256, 256), 256)
            back = lax.dot_general(K[...], W[s, at, :], (((1,), (1,)), ((), ())), preferred_element_type=f32)
            back = (back * SCALE).astype(bf16)
            o_back[:, pl.ds(pl.multiple_of(cols.start + j * 256, 256), 256)] = back[:TOK]
            back_st[b, :, at] = back[TOK:]

        state["out"][n] = send(back_st.at[b], o_back.at[:, cols], core, keep=False)

    for s in order[:6]:
        product(s)
    up_z.wait_recv()
    down_z.wait_recv()
    far_z = (w_send(slot(0, MINUS), slot(0, FAR), hZ[0], up), w_send(slot(0, PLUS), slot(0, FAR), hZ[1], down))
    pair_zm = w_send(slot(0, MINUS), slot(1, MINUS), aZ, pair)
    pair_zp = w_send(slot(0, PLUS), slot(1, PLUS), aZ, pair)
    for s in order[6:]:
        product(s)
    pair_x.wait_recv()
    up_px = w_send(slot(1, ZERO), slot(1, MINUS), aX, up)
    down_px = w_send(slot(1, ZERO), slot(1, PLUS), aX, down)
    forward(own)

    up_x.wait_recv()
    down_x.wait_recv()
    far_x = (w_send(slot(0, MINUS), slot(0, FAR), hX[0], up), w_send(slot(0, PLUS), slot(0, FAR), hX[1], down))
    for copy in y_parts:
        copy.wait_recv()

    @pl.loop(0, 128 // 32)
    def _(r):
        at = pl.ds(pl.multiple_of(r * 32, 32), 32)
        mine = DF[pl.ds(pl.multiple_of(y * 128 + r * 32, 32), 32), :]
        total = (mine + RY[0, at, :]) + (RY[1, at, :] + RY[2, at, :])
        A[at, :] = total.astype(bf16)

    x_sum = send(A, RXH, cross)

    forward(slot(0, PLUS))
    forward(slot(0, MINUS))
    for copy in far_z:
        copy.wait_recv()
    pair_z2 = w_send(slot(0, FAR), slot(1, FAR), aZ, pair)
    pair_z.wait_recv()
    forward(slot(1, ZERO))

    up_px.wait_recv()
    down_px.wait_recv()
    far_px = (w_send(slot(1, MINUS), slot(1, FAR), hPX[0], up), w_send(slot(1, PLUS), slot(1, FAR), hPX[1], down))

    gX, gZ = pl.ds(0, RX), pl.ds(RX, ROWS - RX)
    gx2, gz2 = RX // 2, (ROWS - RX) // 2
    x_parts = [send(G.at[slot(1, dz), gZ], x_own if dz == ZERO else x_zpart.at[dz - 1], pair)
               for dz in (FAR, PLUS, MINUS, ZERO)]
    halves = {}
    for dx in (1, 0):
        halves[dx] = (send(G.at[slot(dx, FAR), pl.ds(0, gx2)], half_x.at[dx, 0], up),
                      send(G.at[slot(dx, FAR), pl.ds(gx2, gx2)], half_x.at[dx, 1], down))

    def add(s, lo, n, *terms):
        @pl.loop(0, n // 16)
        def _(r):
            at = pl.ds(pl.multiple_of(lo + r * 16, 16), 16)
            rows = pl.ds(pl.multiple_of(r * 16, 16), 16)
            total = G[s, at, :].astype(f32)
            for term in terms:
                total += term[rows, :].astype(f32)
            G[s, at, :] = total.astype(bf16)

    fulls = {}

    def x_full(dx):
        halves[dx][0].wait_recv()
        add(slot(dx, PLUS), 0, gx2, half_x.at[dx, 0])
        full = full_pair if dx else full_own
        u = send(G.at[slot(dx, PLUS), gX], full.at[0], up)
        halves[dx][1].wait_recv()
        add(slot(dx, MINUS), gx2, gx2, half_x.at[dx, 1])
        d = send(G.at[slot(dx, MINUS), gX], full.at[1], down)
        fulls[dx] = (u, d)

    for copy in far_x:
        copy.wait_recv()
    forward(slot(0, FAR))
    pair_zm.wait_recv()
    forward(slot(1, MINUS))
    x_sum.wait_recv()

    @pl.loop(0, 128 // 32)
    def _(r):
        at = pl.ds(pl.multiple_of(r * 32, 32), 32)
        total = A[at, :].astype(f32) + RXH[at, :].astype(f32)
        DL[pl.ds(pl.multiple_of(y * 128 + r * 32, 32), 32), :] = total * 0.125

    y_back = [send(DL.at[quarter(y)], DL.at[quarter(y)], ys[k - 1]) for k in (1, 2, 3)]

    pair_zp.wait_recv()
    forward(slot(1, PLUS))
    for copy in far_px:
        copy.wait_recv()
    pair_z2.wait_recv()
    forward(slot(1, FAR))
    keys_swap = send(acc.at[pl.ds(TOK, TOK)], acc_in, core)
    x_full(1)
    x_parts[0].wait_recv()
    add(slot(0, FAR), RX, ROWS - RX, x_zpart.at[FAR - 1])
    z_halves = (send(G.at[slot(0, FAR), pl.ds(RX, gz2)], half_z.at[0], up),
                send(G.at[slot(0, FAR), pl.ds(RX + gz2, gz2)], half_z.at[1], down))
    x_full(0)

    keys_swap.wait_recv()

    @pl.loop(0, TOK // 16)
    def _(r):
        at = pl.ds(pl.multiple_of(r * 16, 16), 16)
        o_keys[at, :] = ((acc[at, :] + acc_in[at, :]) * SCALE).astype(bf16)

    for copy in y_back:
        copy.wait_recv()
    ld_mom.wait()

    @pl.loop(0, ROWS // 16)
    def _(r):
        at = pl.ds(pl.multiple_of(r * 16, 16), 16)
        delta = DL[at, :]
        moment = momentum_coef * M[at, :] + delta
        M[at, :] = moment
        GL[at, :] = GL[at, :] - outer_rate * (momentum_coef * moment + delta)

    x_parts[1].wait_recv()
    x_parts[2].wait_recv()
    add(slot(0, PLUS), RX, ROWS - RX, x_zpart.at[PLUS - 1])
    add(slot(0, MINUS), RX, ROWS - RX, x_zpart.at[MINUS - 1])
    z_halves[0].wait_recv()
    add(slot(0, PLUS), RX, gz2, half_z.at[0])
    u = send(G.at[slot(0, PLUS), gZ], full_z.at[0], up)
    z_halves[1].wait_recv()
    add(slot(0, MINUS), RX + gz2, gz2, half_z.at[1])
    z_fulls = (u, send(G.at[slot(0, MINUS), gZ], full_z.at[1], down))

    for copy in fulls[1]:
        copy.wait_recv()
    add(slot(1, ZERO), 0, RX, full_pair.at[0], full_pair.at[1])
    last = send(G.at[slot(1, ZERO), gX], x_last, pair)

    for copy in fulls[0]:
        copy.wait_recv()
    last.wait_recv()
    x_parts[3].wait_recv()
    for copy in z_fulls:
        copy.wait_recv()
    for n in (6, 7):
        state["out"][n].wait_send()
    for n in range(8):
        state["out"][n].wait_recv()
    for copy in sent:
        copy.wait_send()


def finish(
    keys, back, L, GL, M, g_own, x_own, x_last, full_own, full_z,
    o_keys, o_back, o_merged, o_glob, o_mom, merged, sem,
):
    f32 = jnp.float32
    copies = []

    def move(src, dst):
        copy = pltpu.make_async_copy(src, dst, sem.at[len(copies)])
        copy.start()
        copies.append(copy)

    def merge(lo, n, *terms):
        @pl.loop(0, n // 16)
        def _(r):
            at = pl.ds(pl.multiple_of(lo + r * 16, 16), 16)
            rows = pl.ds(pl.multiple_of(r * 16, 16), 16)
            grad = g_own[at, :].astype(f32)
            for term in terms:
                grad += term[rows, :].astype(f32)
            merged[at, :] = mix_weight * (L[at, :] - inner_rate * grad) + (1.0 - mix_weight) * GL[at, :]

        move(merged.at[pl.ds(lo, n)], o_merged.at[pl.ds(lo, n)])

    move(back, o_back)
    move(M, o_mom)
    move(GL, o_glob)
    move(keys, o_keys)
    merge(0, RX, full_own.at[0], full_own.at[1], x_last)
    merge(RX, ROWS - RX, x_own, full_z.at[0], full_z.at[1])
    for copy in copies:
        copy.wait()


def shards(hidden, key_grad, local_weight, global_weight, momentum):
    bf16, f32 = jnp.bfloat16, jnp.float32
    vm = pltpu.VMEM
    anywhere = pl.BlockSpec(memory_space=pl.ANY)
    inside = pl.BlockSpec(memory_space=pltpu.VMEM)
    held = [
        vm((TOK, KV), bf16),
        vm((TOK, D), bf16),
        vm((ROWS, KV), f32),
        vm((ROWS, KV), f32),
        vm((ROWS, KV), f32),
        vm((ROWS, KV), bf16),
        vm((ROWS - RX, KV), bf16),
        vm((RX, KV), bf16),
        vm((2, RX, KV), bf16),
        vm((2, ROWS - RX, KV), bf16),
    ]
    parts = pl.pallas_call(
        kernel,
        out_shape=held,
        in_specs=[anywhere] * 5,
        out_specs=[inside] * len(held),
        scratch_shapes=[
            vm((8, ROWS, KV), bf16),
            vm((8, 2 * TOK, ROWS), bf16),
            vm((2 * TOK, KV), bf16),
            vm((8, ROWS, KV), bf16),
            vm((2 * TOK, KV), f32),
            vm((TOK, KV), f32),
            vm((2, TOK, ROWS), bf16),
            vm((ROWS, KV), f32),
            vm((3, 128, KV), f32),
            vm((128, KV), bf16),
            vm((128, KV), bf16),
            vm((ROWS, KV), f32),
            vm((3, ROWS - RX, KV), bf16),
            vm((2, 2, RX // 2, KV), bf16),
            vm((2, (ROWS - RX) // 2, KV), bf16),
            vm((2, RX, KV), bf16),
            pltpu.SemaphoreType.DMA((64,)),
            pltpu.SemaphoreType.DMA((64,)),
            pltpu.SemaphoreType.DMA((32,)),
        ],
        compiler_params=pltpu.CompilerParams(
            collective_id=0, has_side_effects=True, vmem_limit_bytes=44 * 2**20
        ),
        cost_estimate=pl.CostEstimate(flops=3 * 2 * TOK * D * KV, bytes_accessed=26 * 2**20, transcendentals=0),
        name="step",
    )(hidden, key_grad, local_weight[0], global_weight, momentum)
    parts = [pltpu.with_memory_space_constraint(a, pltpu.VMEM) for a in parts]
    keys, back, merged, global_next, moment_next = pl.pallas_call(
        finish,
        out_shape=(
            jax.ShapeDtypeStruct((TOK, KV), bf16),
            jax.ShapeDtypeStruct((TOK, D), bf16),
            jax.ShapeDtypeStruct((ROWS, KV), f32),
            jax.ShapeDtypeStruct((ROWS, KV), f32),
            jax.ShapeDtypeStruct((ROWS, KV), f32),
        ),
        in_specs=[inside] * len(held),
        out_specs=[anywhere] * 5,
        scratch_shapes=[vm((ROWS, KV), f32), pltpu.SemaphoreType.DMA((8,))],
        compiler_params=pltpu.CompilerParams(vmem_limit_bytes=8 * 2**20),
        name="finish",
    )(*parts)
    return (keys, back, merged[None], global_next, moment_next)


def solution(mesh):
    placed = (
        P(("worker", "fsdp"), None),
        P(("worker", "fsdp"), None),
        P("worker", "fsdp", None),
        P("fsdp", None),
        P("fsdp", None),
    )
    return jax.shard_map(
        shards,
        mesh=mesh,
        in_specs=placed,
        out_specs=(
            P(("worker", "fsdp"), None),
            P(("worker", "fsdp"), None),
            P("worker", "fsdp", None),
            P("fsdp", None),
            P("fsdp", None),
        ),
        check_vma=False,
    )
```
